32 devices in a mesh: grp: 4 (over y, x), seq: 8 (over z, core).
Axes of the slice: x: 2, y: 2, z: 4, core: 2. Of those that a mesh axis runs over, the one named last changes fastest.
Arguments:
- queries: bfloat16 [4096, 3072], P(('grp', 'seq')), may hold values from -130 to 130
- keys: bfloat16 [4096, 192], P(('grp', 'seq')), may hold values from -6 to 6
- values: bfloat16 [4096, 128], P(('grp', 'seq')), may hold values from -6 to 6
- comp_key_weight: float32 [16, 192], replicated, may hold values from -1.5 to 1.5
- comp_value_weight: float32 [16, 128], replicated, may hold values from -1.5 to 1.5
- select: int32 [64, 16], P(('grp', 'seq')), may hold values from 0 to 63, as said below
- gate_logits: float32 [4096, 48], P(('grp', 'seq')), may hold values from -6 to 6
Outputs:
- attended: bfloat16 [4096, 2048], P(('grp', 'seq'))
The draws below stay inside these ranges and needn't reach their ends.
Inputs may be any that keep to these rules, and one draw needn't show every extreme that they name: select[i, 0] = i; every entry is at most i. Devices are numbered grp index times 8 plus seq index, and a device holds 2 consecutive blocks. Every entry lies on a block held by the tile's own device, by a device of the same group, or by a device of the previous group. Of the tiles of one device, all entries that fall off that device and on devices of one seq index name the same block.
All inputs are finite; a program needn't handle non-finite values.
Results may differ from the reference program's by a relative error of at most 0.0046.
Values may be sent and summed in bfloat16 or wider, within the bound.
A program may use at most 128 MiB of HBM per device.

```python
import jax
import jax.numpy as jnp
from jax import lax

H = 16
DK = 192
DV = 128
STRIDE = 16
BLK = 64
SEL = 16
WINDOW = 512
TOKENS = 4096
NCOMP = 256
TILES_DEV = 2
NTILES = 64
N_SEQ = 8


def common_rows(key):
    base_keys = jax.random.normal(jax.random.fold_in(key, 11), (TOKENS, DK), jnp.float32)
    base_queries = 0.6 * jax.random.normal(jax.random.fold_in(key, 12), (TOKENS, H, DK), jnp.float32)
    return (jnp.clip(base_queries, -130.0, 130.0), jnp.clip(base_keys, -6.0, 6.0))


def draw_queries(key, part):
    return common_rows(key)[0].reshape(TOKENS, H * DK).astype(jnp.bfloat16)


def draw_keys(key, part):
    return common_rows(key)[1].astype(jnp.bfloat16)


def draw_select(key, part):
    tile_ids = jnp.arange(NTILES, dtype=jnp.int32)
    owner_dev = tile_ids // TILES_DEV
    device_count = NTILES // TILES_DEV
    owner_grp = owner_dev // N_SEQ
    owner_seq = owner_dev % N_SEQ
    offset_table = jax.random.randint(jax.random.fold_in(key, 21), (device_count, N_SEQ), 0, TILES_DEV)
    coin_table = jax.random.randint(jax.random.fold_in(key, 24), (device_count, N_SEQ), 0, 2)
    rotation = jax.random.randint(jax.random.fold_in(key, 25), (device_count,), 0, N_SEQ - 1)
    own_pick = jax.random.randint(jax.random.fold_in(key, 23), (NTILES, SEL - 1), 0, (tile_ids % TILES_DEV)[:, None] + 1)
    pick_number = (tile_ids % TILES_DEV)[:, None] * (SEL - 1) + jnp.arange(SEL - 1, dtype=jnp.int32)[None, :]
    peer = (owner_seq[:, None] + 1 + (pick_number + rotation[owner_dev][:, None]) % (N_SEQ - 1)) % N_SEQ
    coin = coin_table[owner_dev[:, None], peer]
    use_prior = (peer > owner_seq[:, None]) | (coin == 1)
    source_grp = jnp.where(use_prior, owner_grp[:, None] - 1, owner_grp[:, None])
    valid = source_grp >= 0
    source_dev = source_grp * N_SEQ + peer
    far_block = source_dev * TILES_DEV + offset_table[owner_dev[:, None], peer]
    near_block = owner_dev[:, None] * TILES_DEV + own_pick
    remaining = jnp.where(valid, far_block, near_block)
    return jnp.concatenate([tile_ids[:, None], remaining], 1).astype(jnp.int32)


def block_levels(rng, shape, shards, low, largest):
    gain, own = 1.0, jax.random.fold_in(rng, 6)
    for dim, blocks in shards:
        steps = jnp.exp(jax.random.uniform(jax.random.fold_in(own, dim), (blocks,), jnp.float32, low / len(shards), largest / len(shards)))
        gain = gain * jnp.repeat(steps, shape[dim] // blocks).reshape([-1 if axis == dim else 1 for axis in range(len(shape))])
    return gain


def bell_draw(own_key, extent, scale, reach, split=(), kind=jnp.bfloat16):
    entries = scale * jax.random.normal(own_key, extent, jnp.float32)
    if split:
        entries = entries * block_levels(own_key, extent, split, -0.22, 0.18)
    return jnp.clip(entries, -reach, reach).astype(kind)


def setup_inputs(seed: int = 0) -> dict:
    streams_of = jax.random.split(jax.random.key(seed), 8)
    queries = draw_queries(jax.random.fold_in(streams_of[7], 71), 0)
    keys = draw_keys(jax.random.fold_in(streams_of[7], 71), 0)
    values = bell_draw(streams_of[2], (TOKENS, DV), 1.0, 6.0, ((0, 32),))
    comp_key_weight = bell_draw(streams_of[3], (STRIDE, DK), 0.25, 1.5, (), jnp.float32)
    comp_value_weight = bell_draw(streams_of[4], (STRIDE, DV), 0.25, 1.5, (), jnp.float32)
    select = draw_select(jax.random.fold_in(streams_of[7], 71), 0)
    gate_logits = bell_draw(streams_of[6], (TOKENS, 3 * H), 1.5, 6.0, ((0, 32),), jnp.float32)
    return dict(queries=queries, keys=keys, values=values, comp_key_weight=comp_key_weight, comp_value_weight=comp_value_weight, select=select, gate_logits=gate_logits)


def normalize(scores, allowed):
    scores = jnp.where(allowed, scores, -jnp.inf)
    highest = jnp.max(scores, axis=-1, keepdims=True)
    weights = jnp.exp(scores - highest)
    return (weights / jnp.sum(weights, axis=-1, keepdims=True)).astype(jnp.bfloat16)


def compress(source, weight):
    shaped = source.astype(jnp.float32).reshape(-1, STRIDE, source.shape[1])
    return jnp.sum(shaped * weight[None], axis=1)


def reference(queries, keys, values, comp_key_weight, comp_value_weight, select, gate_logits):
    score_scale = DK ** -0.5
    highest = lax.Precision.HIGHEST
    comp_keys = compress(keys, comp_key_weight)
    comp_values = compress(values, comp_value_weight)
    comp_starts = jnp.arange(NCOMP, dtype=jnp.int32) * STRIDE
    padded_keys = jnp.concatenate([jnp.zeros((WINDOW, DK), keys.dtype), keys], 0)
    padded_values = jnp.concatenate([jnp.zeros((WINDOW, DV), values.dtype), values], 0)
    offsets = jnp.arange(BLK, dtype=jnp.int32)
    window_span = jnp.arange(WINDOW + BLK - 1, dtype=jnp.int32)

    def one_tile(tile_id):
        first_row = tile_id * BLK
        row_block = lax.dynamic_slice_in_dim(queries, first_row, BLK, 0).astype(jnp.float32).reshape(BLK, H, DK)
        places = first_row + offsets
        comp_scores = jnp.einsum("thd,jd->thj", row_block, comp_keys, precision=highest) * score_scale
        comp_weights = normalize(comp_scores, comp_starts[None, None, :] <= places[:, None, None])
        comp_out = jnp.einsum("thj,jv->thv", comp_weights.astype(jnp.float32), comp_values, precision=highest)
        picked = select[tile_id]
        key_places = (picked[:, None] * BLK + offsets[None, :]).reshape(-1).astype(jnp.int32)
        sel_keys = jnp.take(keys, key_places, axis=0).astype(jnp.float32)
        sel_values = jnp.take(values, key_places, axis=0).astype(jnp.float32)
        sel_scores = jnp.einsum("thd,kd->thk", row_block, sel_keys) * score_scale
        sel_weights = normalize(sel_scores, key_places[None, None, :] <= places[:, None, None])
        sel_out = jnp.einsum("thk,kv->thv", sel_weights.astype(jnp.float32), sel_values)
        win_keys = lax.dynamic_slice_in_dim(padded_keys, first_row + 1, WINDOW + BLK - 1, 0).astype(jnp.float32)
        win_values = lax.dynamic_slice_in_dim(padded_values, first_row + 1, WINDOW + BLK - 1, 0).astype(jnp.float32)
        win_places = first_row - WINDOW + 1 + window_span
        later = win_places[None, None, :]
        allowed = (later <= places[:, None, None]) & (later > places[:, None, None] - WINDOW) & (later >= 0)
        win_scores = jnp.einsum("thd,kd->thk", row_block, win_keys) * score_scale
        win_out = jnp.einsum("thk,kv->thv", normalize(win_scores, allowed).astype(jnp.float32), win_values)
        branch_gates = jax.nn.sigmoid(lax.dynamic_slice_in_dim(gate_logits, first_row, BLK, 0)).reshape(BLK, 3, H)
        combined = branch_gates[:, 0, :, None] * comp_out + branch_gates[:, 1, :, None] * sel_out
        combined = combined + branch_gates[:, 2, :, None] * win_out
        return combined.astype(jnp.bfloat16).reshape(BLK, H * DV)

    return lax.map(one_tile, jnp.arange(NTILES, dtype=jnp.int32)).reshape(TOKENS, H * DV)
```

```python
import functools

import jax
import jax.numpy as jnp
from jax import lax
from jax.experimental import pallas as pl
from jax.experimental.pallas import tpu as pltpu
from jax.sharding import PartitionSpec as P

WINDOW = 512
LANES = 128
MESH = pl.DeviceIdType.MESH


def padded(width):
    return -(-width // LANES) * LANES


def exchange_kernel(
    groups, within, keys, values, key_weight, value_weight, table, comp,
    packed, comp_own, recv_rows, recv_comp, along_rows, along_comp,
    pair_rows, pair_comp, next_rows, next_comp, local_sem,
):
    group = lax.axis_index("grp")
    seq = lax.axis_index("seq")
    half = within // 2
    sibling = seq + 1 - 2 * lax.rem(seq, 2)
    key_dim = keys.shape[1]
    value_dim = values.shape[1]
    key_room = padded(key_dim)
    stride = key_weight.shape[0]
    comp_rows = keys.shape[0] // stride

    def same_parity(distance):
        return lax.rem(seq + 2 * distance + 2 * within, within)

    barrier = pltpu.get_barrier_semaphore()

    def greet(distance, carry):
        pl.semaphore_signal(
            barrier, inc=1, device_id=(group, same_parity(distance)), device_id_type=MESH
        )
        return carry

    lax.fori_loop(1, half, greet, 0)
    pl.semaphore_signal(barrier, inc=1, device_id=(group, sibling), device_id_type=MESH)
    for step in range(1, groups):
        other = lax.rem(group + step, groups)
        pl.semaphore_signal(barrier, inc=1, device_id=(other, seq), device_id_type=MESH)

    packed[:, :key_room] = jnp.zeros((keys.shape[0], key_room), packed.dtype)
    packed[:, :key_dim] = keys[...]
    packed[:, key_room:] = values[...]
    comp_own[...] = jnp.zeros_like(comp_own)

    def summed(source, weight):
        wide = source[...].astype(jnp.float32).reshape(comp_rows, stride, source.shape[1])
        return jnp.sum(wide * weight[...][None], axis=1)

    comp_own[:, :key_dim] = summed(keys, key_weight)
    comp_own[:, key_room:] = summed(values, value_weight)
    pl.semaphore_wait(barrier, half - 1 + 1 + groups - 1)

    def rows_copy(source, slot, send_sem, target):
        return pltpu.make_async_remote_copy(
            src_ref=source, dst_ref=table.at[slot], send_sem=send_sem,
            recv_sem=recv_rows.at[slot], device_id=target, device_id_type=MESH,
        )

    def comp_copy(source, slot, send_sem, target):
        return pltpu.make_async_remote_copy(
            src_ref=source, dst_ref=comp.at[slot], send_sem=send_sem,
            recv_sem=recv_comp.at[slot], device_id=target, device_id_type=MESH,
        )

    own_slot = within + seq
    own_comp = group * within + seq

    def to_next_groups(rows_source, comp_source, member):
        @pl.when(group < groups - 1)
        def _():
            rows_copy(rows_source, member, next_rows.at[member], (group + 1, seq)).start()

        for step in range(1, groups):
            @pl.when(group + step < groups)
            def _():
                comp_copy(
                    comp_source, group * within + member,
                    next_comp.at[step * within + member], (group + step, seq),
                ).start()

    def spread(distance, carry):
        target = (group, same_parity(distance))
        rows_copy(packed, own_slot, along_rows.at[distance], target).start()
        comp_copy(comp_own, own_comp, along_comp.at[distance], target).start()
        return carry

    lax.fori_loop(1, half, spread, 0)
    to_next_groups(packed, comp_own, seq)
    rows_copy(packed, own_slot, pair_rows.at[own_slot], (group, sibling)).start()
    comp_copy(comp_own, own_comp, pair_comp.at[own_comp], (group, sibling)).start()
    keep_rows = pltpu.make_async_copy(packed, table.at[own_slot], local_sem.at[0])
    keep_comp = pltpu.make_async_copy(comp_own, comp.at[own_comp], local_sem.at[1])
    keep_rows.start()
    keep_comp.start()

    def arrive_rows(slot):
        rows_copy(packed, slot, pair_rows.at[slot], (group, sibling)).wait_recv()

    def arrive_comp(slot):
        comp_copy(comp_own, slot, pair_comp.at[slot], (group, sibling)).wait_recv()

    def pass_rows(slot):
        arrive_rows(slot)
        rows_copy(table.at[slot], slot, pair_rows.at[slot], (group, sibling)).start()

    def pass_comp(slot):
        arrive_comp(slot)
        comp_copy(comp.at[slot], slot, pair_comp.at[slot], (group, sibling)).start()

    def relay(distance, carry):
        member = same_parity(-distance)
        slot = within + member
        comp_slot = group * within + member
        arrive_rows(slot)
        arrive_comp(comp_slot)
        to_next_groups(table.at[slot], comp.at[comp_slot], member)
        rows_copy(table.at[slot], slot, pair_rows.at[slot], (group, sibling)).start()
        comp_copy(comp.at[comp_slot], comp_slot, pair_comp.at[comp_slot], (group, sibling)).start()
        return carry

    lax.fori_loop(1, half, relay, 0)

    def relay_prior(distance, carry):
        member = same_parity(-distance)

        @pl.when(group > 0)
        def _():
            pass_rows(member)

        for step in range(1, groups):
            @pl.when(group >= step)
            def _():
                pass_comp((group - step) * within + member)

        return carry

    lax.fori_loop(0, half, relay_prior, 0)

    def finish(distance, carry):
        member = same_parity(distance)
        other = member + sibling - seq
        arrive_rows(within + other)
        arrive_comp(group * within + other)
        rows_copy(packed, within + member, pair_rows.at[within + member], (group, sibling)).wait_send()
        comp_copy(
            comp_own, group * within + member, pair_comp.at[group * within + member], (group, sibling)
        ).wait_send()

        @pl.when(group > 0)
        def _():
            arrive_rows(other)
            rows_copy(packed, member, pair_rows.at[member], (group, sibling)).wait_send()

        for step in range(1, groups):
            @pl.when(group >= step)
            def _():
                arrive_comp((group - step) * within + other)
                slot = (group - step) * within + member
                comp_copy(comp_own, slot, pair_comp.at[slot], (group, sibling)).wait_send()

        @pl.when(group < groups - 1)
        def _():
            rows_copy(packed, member, next_rows.at[member], (group + 1, seq)).wait_send()

        for step in range(1, groups):
            @pl.when(group + step < groups)
            def _():
                comp_copy(
                    comp_own, group * within + member,
                    next_comp.at[step * within + member], (group + step, seq),
                ).wait_send()

        return carry

    lax.fori_loop(0, half, finish, 0)

    def sent(distance, carry):
        target = (group, same_parity(distance))
        rows_copy(packed, own_slot, along_rows.at[distance], target).wait_send()
        comp_copy(comp_own, own_comp, along_comp.at[distance], target).wait_send()
        return carry

    lax.fori_loop(1, half, sent, 0)
    keep_rows.wait()
    keep_comp.wait()


def exchange(groups, within, keys, values, key_weight, value_weight):
    length, key_dim = keys.shape
    width = padded(key_dim) + padded(values.shape[1])
    comp_rows = length // key_weight.shape[0]
    dma = pltpu.SemaphoreType.DMA
    vmem = pl.BlockSpec(memory_space=pltpu.VMEM)
    return pl.pallas_call(
        functools.partial(exchange_kernel, groups, within),
        out_shape=(
            jax.ShapeDtypeStruct((2 * within, length, width), keys.dtype),
            jax.ShapeDtypeStruct((groups * within, comp_rows, width), jnp.float32),
        ),
        in_specs=[vmem] * 4,
        out_specs=(pl.BlockSpec(memory_space=pl.ANY), pl.BlockSpec(memory_space=pl.ANY)),
        scratch_shapes=[
            pltpu.VMEM((length, width), keys.dtype),
            pltpu.VMEM((comp_rows, width), jnp.float32),
            dma((2 * within,)),
            dma((groups * within,)),
            dma((within,)),
            dma((within,)),
            dma((2 * within,)),
            dma((groups * within,)),
            dma((within,)),
            dma((groups * within,)),
            dma((2,)),
        ],
        compiler_params=pltpu.CompilerParams(collective_id=0, has_side_effects=True),
        name="exchange",
    )(keys, values, key_weight, value_weight)


def contract(left, right):
    return lax.dot_general(left, right, (((1,), (1,)), ((), ())), preferred_element_type=jnp.float32)


def attend_kernel(
    within, stride, key_dim, heads_step, place, select, queries, gate_logits, table, comp, out,
    rows, gates, sel_keys, sel_values, win_values, comp_parts, comp_high, comp_low,
    sel_bias, win_bias, comp_bias,
):
    group, seq = place[0], place[1]
    length = queries.shape[0]
    tiles, picks = select.shape
    block = length // tiles
    heads = gate_logits.shape[1] // 3
    value_dim = out.shape[1] // heads
    key_room = padded(key_dim)
    comp_count = comp.shape[0]
    group_len = within * length
    win_len = win_bias.shape[1]
    first_place = (group - 1) * group_len
    factor = key_dim ** (-0.5) * 1.4426950408889634
    low = -jnp.inf

    @pl.when(group == 0)
    def _():
        table[:group_len, :] = jnp.zeros((group_len, table.shape[1]), table.dtype)

    comp_here = (lax.broadcasted_iota(jnp.int32, (comp_count, 1), 0) * stride) < (group + 1) * group_len
    source = jnp.where(comp_here, comp[...], 0.0)
    rest = source[:, :key_dim]
    for part in range(3):
        piece = rest.astype(jnp.bfloat16)
        comp_parts[part] = piece
        rest = rest - piece.astype(jnp.float32)
    value_part = source[:, key_room:]
    high = value_part.astype(jnp.bfloat16)
    comp_high[:, :value_dim] = high
    comp_high[:, value_dim:] = jnp.ones((comp_count, LANES), jnp.bfloat16)
    comp_low[...] = (value_part - high.astype(jnp.float32)).astype(jnp.bfloat16)
    sel_values[:, value_dim:] = jnp.ones((picks * block, LANES), jnp.bfloat16)
    win_values[:, value_dim:] = jnp.ones((win_len, LANES), jnp.bfloat16)
    gate_all = jax.nn.sigmoid(gate_logits[...])
    step_rows = heads_step * block

    for tile in range(tiles):
        top = tile * block
        tile_place = (group * within + seq) * length + top
        for head in range(heads):
            rows[head * block : (head + 1) * block, :] = queries[
                top : top + block, head * key_dim : (head + 1) * key_dim
            ]
            for branch in range(3):
                column = branch * heads + head
                gates[branch, head * block : (head + 1) * block, :] = jnp.broadcast_to(
                    gate_all[top : top + block, column : column + 1], (block, LANES)
                )
        for pick in range(picks):
            start = pl.multiple_of(select[tile, pick] * block - first_place, block)
            got = table[pl.ds(start, block), :]
            sel_keys[pick * block : (pick + 1) * block, :] = got[:, :key_room]
            sel_values[pick * block : (pick + 1) * block, :value_dim] = got[:, key_room:]
        lane_all = lax.broadcasted_iota(jnp.int32, (block, picks * block), 1)
        row_place = tile_place + lax.broadcasted_iota(jnp.int32, (block, picks * block), 0)
        shift = jnp.zeros((1, picks * block), jnp.int32)
        lane_one = lax.broadcasted_iota(jnp.int32, (1, picks * block), 1)
        for pick in range(picks):
            inside = (lane_one >= pick * block) & (lane_one < (pick + 1) * block)
            shift = jnp.where(inside, (select[tile, pick] - pick) * block, shift)
        sel_bias[...] = jnp.where(lane_all + shift <= row_place, 0.0, low)
        win_start = pl.multiple_of(group_len + seq * length + top - (win_len - block), block)
        win_place = tile_place - (win_len - block) + lax.broadcasted_iota(jnp.int32, (block, win_len), 1)
        win_row = tile_place + lax.broadcasted_iota(jnp.int32, (block, win_len), 0)
        win_bias[...] = jnp.where(
            (win_place <= win_row) & (win_place > win_row - WINDOW) & (win_place >= 0), 0.0, low
        )
        comp_place = stride * lax.broadcasted_iota(jnp.int32, (block, comp_count), 1)
        comp_row = tile_place + lax.broadcasted_iota(jnp.int32, (block, comp_count), 0)
        comp_bias[...] = jnp.where(comp_place <= comp_row, 0.0, low)
        win_values[:, :value_dim] = table[pl.ds(win_start, win_len), key_room:]

        def weigh(scores, bias):
            scores = scores.reshape(heads_step, block, scores.shape[1]) + bias[...][None]
            top_score = jnp.max(scores, axis=-1, keepdims=True)
            weights = jnp.exp2((scores - top_score) * factor)
            return weights.astype(jnp.bfloat16).reshape(step_rows, scores.shape[2])

        def mix(weights, extended):
            both = jnp.dot(weights, extended, preferred_element_type=jnp.float32)
            return both[:, :value_dim], both[:, value_dim : value_dim + value_dim]

        def some_heads(step, carry):
            here = pl.ds(pl.multiple_of(step * step_rows, step_rows), step_rows)
            query = rows[here, :]
            weights = weigh(contract(query, sel_keys[:, :key_dim]), sel_bias)
            numer, denom = mix(weights, sel_values[...])
            total = gates[1, here, :] * numer / denom
            weights = weigh(contract(query, table[pl.ds(win_start, win_len), :key_dim]), win_bias)
            numer, denom = mix(weights, win_values[...])
            total = total + gates[2, here, :] * numer / denom
            scores = (
                contract(query, comp_parts[0]) + contract(query, comp_parts[1])
            ) + contract(query, comp_parts[2])
            weights = weigh(scores, comp_bias)
            numer, denom = mix(weights, comp_high[...])
            numer = numer + jnp.dot(weights, comp_low[...], preferred_element_type=jnp.float32)
            total = (total + gates[0, here, :] * numer / denom).astype(out.dtype)
            pieces = [total[n * block : (n + 1) * block, :] for n in range(heads_step)]
            columns = pl.ds(pl.multiple_of(step * heads_step * value_dim, LANES), heads_step * value_dim)
            out[top : top + block, columns] = jnp.concatenate(pieces, axis=1)
            return carry

        lax.fori_loop(0, heads // heads_step, some_heads, 0)


def attend(within, stride, key_dim, place, select, queries, gate_logits, table, comp):
    length = queries.shape[0]
    tiles, picks = select.shape
    block = length // tiles
    heads = gate_logits.shape[1] // 3
    value_dim = table.shape[1] - padded(key_dim)
    comp_count = comp.shape[0]
    win_len = WINDOW + block
    sel_len = picks * block
    vmem = pl.BlockSpec(memory_space=pltpu.VMEM)
    smem = pl.BlockSpec(memory_space=pltpu.SMEM)
    bf16, f32 = jnp.bfloat16, jnp.float32
    return pl.pallas_call(
        functools.partial(attend_kernel, within, stride, key_dim, 4),
        out_shape=jax.ShapeDtypeStruct((length, heads * value_dim), queries.dtype),
        in_specs=[smem, smem, vmem, vmem, vmem, vmem],
        out_specs=vmem,
        scratch_shapes=[
            pltpu.VMEM((heads * block, key_dim), bf16),
            pltpu.VMEM((3, heads * block, LANES), f32),
            pltpu.VMEM((sel_len, padded(key_dim)), bf16),
            pltpu.VMEM((sel_len, value_dim + LANES), bf16),
            pltpu.VMEM((win_len, value_dim + LANES), bf16),
            pltpu.VMEM((3, comp_count, key_dim), bf16),
            pltpu.VMEM((comp_count, value_dim + LANES), bf16),
            pltpu.VMEM((comp_count, value_dim), bf16),
            pltpu.VMEM((block, sel_len), f32),
            pltpu.VMEM((block, win_len), f32),
            pltpu.VMEM((block, comp_count), f32),
        ],
        compiler_params=pltpu.CompilerParams(vmem_limit_bytes=56 * 1024 * 1024),
        name="attend",
    )(place, select, queries, gate_logits, table, comp)


def shards(queries, keys, values, comp_key_weight, comp_value_weight, select, gate_logits):
    groups = lax.axis_size("grp")
    within = lax.axis_size("seq")
    place = jnp.stack([lax.axis_index("grp"), lax.axis_index("seq")]).astype(jnp.int32)
    table, comp = exchange(groups, within, keys, values, comp_key_weight, comp_value_weight)
    table = table.reshape(-1, table.shape[2])
    comp = comp.reshape(-1, comp.shape[2])
    return attend(
        within, comp_key_weight.shape[0], keys.shape[1], place, select, queries, gate_logits, table, comp
    )


def solution(mesh):
    return jax.shard_map(
        shards,
        mesh=mesh,
        in_specs=(
            P(("grp", "seq"), None),
            P(("grp", "seq"), None),
            P(("grp", "seq"), None),
            P(),
            P(),
            P(("grp", "seq"), None),
            P(("grp", "seq"), None),
        ),
        out_specs=P(("grp", "seq"), None),
        check_vma=False,
    )
```

```python
import functools

import jax
import jax.numpy as jnp
from jax import lax
from jax.experimental import pallas as pl
from jax.experimental.pallas import tpu as pltpu
from jax.sharding import PartitionSpec as P

WINDOW = 512
LANES = 128
MESH = pl.DeviceIdType.MESH


def padded(width):
    return -(-width // LANES) * LANES


def exchange_kernel(
    groups, within, keys_turned, values, key_weight, value_weight, table, comp,
    packed, comp_own, recv_rows, recv_comp, along_rows, along_comp,
    pair_rows, pair_comp, next_rows, next_comp, local_sem,
):
    group = lax.axis_index("grp")
    seq = lax.axis_index("seq")
    half = within // 2
    sibling = seq + 1 - 2 * lax.rem(seq, 2)
    length = values.shape[0]
    key_dim = keys_turned.shape[0]
    key_room = padded(key_dim)
    stride = key_weight.shape[0]
    comp_rows = length // stride

    def same_parity(distance):
        return lax.rem(seq + 2 * distance + 2 * within, within)

    barrier = pltpu.get_barrier_semaphore()

    def greet(distance, carry):
        pl.semaphore_signal(
            barrier, inc=1, device_id=(group, same_parity(distance)), device_id_type=MESH
        )
        return carry

    lax.fori_loop(1, half, greet, 0)
    pl.semaphore_signal(barrier, inc=1, device_id=(group, sibling), device_id_type=MESH)
    for step in range(1, groups):
        other = lax.rem(group + step, groups)
        pl.semaphore_signal(barrier, inc=1, device_id=(other, seq), device_id_type=MESH)

    keys = keys_turned[...].T
    packed[:, :key_room] = jnp.zeros((length, key_room), packed.dtype)
    packed[:, :key_dim] = keys
    packed[:, key_room:] = values[...]
    comp_own[...] = jnp.zeros_like(comp_own)

    def summed(source, weight):
        wide = source.astype(jnp.float32).reshape(comp_rows, stride, source.shape[1])
        return jnp.sum(wide * weight[...][None], axis=1)

    comp_own[:, :key_dim] = summed(keys, key_weight)
    comp_own[:, key_room:] = summed(values[...], value_weight)
    pl.semaphore_wait(barrier, half - 1 + 1 + groups - 1)

    def rows_copy(source, slot, send_sem, target):
        return pltpu.make_async_remote_copy(
            src_ref=source, dst_ref=table.at[slot], send_sem=send_sem,
            recv_sem=recv_rows.at[slot], device_id=target, device_id_type=MESH,
        )

    def comp_copy(source, slot, send_sem, target):
        return pltpu.make_async_remote_copy(
            src_ref=source, dst_ref=comp.at[slot], send_sem=send_sem,
            recv_sem=recv_comp.at[slot], device_id=target, device_id_type=MESH,
        )

    own_slot = within + seq
    own_comp = group * within + seq

    def to_next_groups(rows_source, comp_source, member):
        @pl.when(group < groups - 1)
        def _():
            rows_copy(rows_source, member, next_rows.at[member], (group + 1, seq)).start()

        for step in range(1, groups):
            @pl.when(group + step < groups)
            def _():
                comp_copy(
                    comp_source, group * within + member,
                    next_comp.at[step * within + member], (group + step, seq),
                ).start()

    def spread(distance, carry):
        target = (group, same_parity(distance))
        rows_copy(packed, own_slot, along_rows.at[distance], target).start()
        comp_copy(comp_own, own_comp, along_comp.at[distance], target).start()
        return carry

    lax.fori_loop(1, half, spread, 0)
    to_next_groups(packed, comp_own, seq)
    rows_copy(packed, own_slot, pair_rows.at[own_slot], (group, sibling)).start()
    comp_copy(comp_own, own_comp, pair_comp.at[own_comp], (group, sibling)).start()
    keep_rows = pltpu.make_async_copy(packed, table.at[own_slot], local_sem.at[0])
    keep_comp = pltpu.make_async_copy(comp_own, comp.at[own_comp], local_sem.at[1])
    keep_rows.start()
    keep_comp.start()

    def arrive_rows(slot):
        rows_copy(packed, slot, pair_rows.at[slot], (group, sibling)).wait_recv()

    def arrive_comp(slot):
        comp_copy(comp_own, slot, pair_comp.at[slot], (group, sibling)).wait_recv()

    def pass_rows(slot):
        arrive_rows(slot)
        rows_copy(table.at[slot], slot, pair_rows.at[slot], (group, sibling)).start()

    def pass_comp(slot):
        arrive_comp(slot)
        comp_copy(comp.at[slot], slot, pair_comp.at[slot], (group, sibling)).start()

    def relay(distance, carry):
        member = same_parity(-distance)
        slot = within + member
        comp_slot = group * within + member
        arrive_rows(slot)
        arrive_comp(comp_slot)
        to_next_groups(table.at[slot], comp.at[comp_slot], member)
        rows_copy(table.at[slot], slot, pair_rows.at[slot], (group, sibling)).start()
        comp_copy(comp.at[comp_slot], comp_slot, pair_comp.at[comp_slot], (group, sibling)).start()
        return carry

    lax.fori_loop(1, half, relay, 0)

    def relay_prior(distance, carry):
        member = same_parity(-distance)

        @pl.when(group > 0)
        def _():
            pass_rows(member)

        for step in range(1, groups):
            @pl.when(group >= step)
            def _():
                pass_comp((group - step) * within + member)

        return carry

    lax.fori_loop(0, half, relay_prior, 0)

    def finish(distance, carry):
        member = same_parity(distance)
        other = member + sibling - seq
        arrive_rows(within + other)
        arrive_comp(group * within + other)
        rows_copy(packed, within + member, pair_rows.at[within + member], (group, sibling)).wait_send()
        comp_copy(
            comp_own, group * within + member, pair_comp.at[group * within + member], (group, sibling)
        ).wait_send()

        @pl.when(group > 0)
        def _():
            arrive_rows(other)
            rows_copy(packed, member, pair_rows.at[member], (group, sibling)).wait_send()

        for step in range(1, groups):
            @pl.when(group >= step)
            def _():
                arrive_comp((group - step) * within + other)
                slot = (group - step) * within + member
                comp_copy(comp_own, slot, pair_comp.at[slot], (group, sibling)).wait_send()

        @pl.when(group < groups - 1)
        def _():
            rows_copy(packed, member, next_rows.at[member], (group + 1, seq)).wait_send()

        for step in range(1, groups):
            @pl.when(group + step < groups)
            def _():
                comp_copy(
                    comp_own, group * within + member,
                    next_comp.at[step * within + member], (group + step, seq),
                ).wait_send()

        return carry

    lax.fori_loop(0, half, finish, 0)

    def sent(distance, carry):
        target = (group, same_parity(distance))
        rows_copy(packed, own_slot, along_rows.at[distance], target).wait_send()
        comp_copy(comp_own, own_comp, along_comp.at[distance], target).wait_send()
        return carry

    lax.fori_loop(1, half, sent, 0)
    keep_rows.wait()
    keep_comp.wait()


def exchange(groups, within, keys, values, key_weight, value_weight):
    length, key_dim = keys.shape
    width = padded(key_dim) + padded(values.shape[1])
    comp_rows = length // key_weight.shape[0]
    dma = pltpu.SemaphoreType.DMA
    vmem = pl.BlockSpec(memory_space=pltpu.VMEM)
    return pl.pallas_call(
        functools.partial(exchange_kernel, groups, within),
        out_shape=(
            jax.ShapeDtypeStruct((2 * within, length, width), keys.dtype),
            jax.ShapeDtypeStruct((groups * within, comp_rows, width), jnp.float32),
        ),
        in_specs=[vmem] * 4,
        out_specs=(pl.BlockSpec(memory_space=pl.ANY), pl.BlockSpec(memory_space=pl.ANY)),
        scratch_shapes=[
            pltpu.VMEM((length, width), keys.dtype),
            pltpu.VMEM((comp_rows, width), jnp.float32),
            dma((2 * within,)),
            dma((groups * within,)),
            dma((within,)),
            dma((within,)),
            dma((2 * within,)),
            dma((groups * within,)),
            dma((within,)),
            dma((groups * within,)),
            dma((2,)),
        ],
        compiler_params=pltpu.CompilerParams(collective_id=0, has_side_effects=True),
        name="exchange",
    )(keys.T, values, key_weight, value_weight)


def contract(left, right):
    return lax.dot_general(left, right, (((1,), (1,)), ((), ())), preferred_element_type=jnp.float32)


def attend_kernel(
    within, stride, key_dim, heads_step, select, queries, gate_logits, table, comp, out,
    rows, gates, sel_keys, sel_values, win_values, comp_parts, comp_high, comp_low,
    sel_bias, win_bias, comp_bias,
):
    group, seq = lax.axis_index("grp"), lax.axis_index("seq")
    length = queries.shape[0]
    tiles, picks = select.shape
    block = length // tiles
    heads = gate_logits.shape[0] // 3
    value_dim = out.shape[1] // heads
    key_room = padded(key_dim)
    comp_count = comp.shape[0]
    group_len = within * length
    win_len = win_bias.shape[1]
    first_place = (group - 1) * group_len
    factor = key_dim ** (-0.5) * 1.4426950408889634
    low = -jnp.inf

    @pl.when(group == 0)
    def _():
        table[:group_len, :] = jnp.zeros((group_len, table.shape[1]), table.dtype)

    comp_here = (lax.broadcasted_iota(jnp.int32, (comp_count, 1), 0) * stride) < (group + 1) * group_len
    source = jnp.where(comp_here, comp[...], 0.0)
    rest = source[:, :key_dim]
    for part in range(3):
        piece = rest.astype(jnp.bfloat16)
        comp_parts[part] = piece
        rest = rest - piece.astype(jnp.float32)
    value_part = source[:, key_room:]
    high = value_part.astype(jnp.bfloat16)
    comp_high[:, :value_dim] = high
    comp_high[:, value_dim:] = jnp.ones((comp_count, LANES), jnp.bfloat16)
    comp_low[...] = (value_part - high.astype(jnp.float32)).astype(jnp.bfloat16)
    sel_values[:, value_dim:] = jnp.ones((picks * block, LANES), jnp.bfloat16)
    win_values[:, value_dim:] = jnp.ones((win_len, LANES), jnp.bfloat16)
    gate_all = jax.nn.sigmoid(gate_logits[...]).T
    step_rows = heads_step * block

    for tile in range(tiles):
        top = tile * block
        tile_place = (group * within + seq) * length + top
        for head in range(heads):
            rows[head * block : (head + 1) * block, :] = queries[
                top : top + block, head * key_dim : (head + 1) * key_dim
            ]
            for branch in range(3):
                column = branch * heads + head
                gates[branch, head * block : (head + 1) * block, :] = jnp.broadcast_to(
                    gate_all[top : top + block, column : column + 1], (block, LANES)
                )
        for pick in range(picks):
            start = pl.multiple_of(select[tile, pick] * block - first_place, block)
            got = table[pl.ds(start, block), :]
            sel_keys[pick * block : (pick + 1) * block, :] = got[:, :key_room]
            sel_values[pick * block : (pick + 1) * block, :value_dim] = got[:, key_room:]
        lane_all = lax.broadcasted_iota(jnp.int32, (block, picks * block), 1)
        row_place = tile_place + lax.broadcasted_iota(jnp.int32, (block, picks * block), 0)
        shift = jnp.zeros((1, picks * block), jnp.int32)
        lane_one = lax.broadcasted_iota(jnp.int32, (1, picks * block), 1)
        for pick in range(picks):
            inside = (lane_one >= pick * block) & (lane_one < (pick + 1) * block)
            shift = jnp.where(inside, (select[tile, pick] - pick) * block, shift)
        sel_bias[...] = jnp.where(lane_all + shift <= row_place, 0.0, low)
        win_start = pl.multiple_of(group_len + seq * length + top - (win_len - block), block)
        win_place = tile_place - (win_len - block) + lax.broadcasted_iota(jnp.int32, (block, win_len), 1)
        win_row = tile_place + lax.broadcasted_iota(jnp.int32, (block, win_len), 0)
        win_bias[...] = jnp.where(
            (win_place <= win_row) & (win_place > win_row - WINDOW) & (win_place >= 0), 0.0, low
        )
        comp_place = stride * lax.broadcasted_iota(jnp.int32, (block, comp_count), 1)
        comp_row = tile_place + lax.broadcasted_iota(jnp.int32, (block, comp_count), 0)
        comp_bias[...] = jnp.where(comp_place <= comp_row, 0.0, low)
        win_values[:, :value_dim] = table[pl.ds(win_start, win_len), key_room:]

        def weigh(scores, bias):
            scores = scores.reshape(heads_step, block, scores.shape[1]) + bias[...][None]
            top_score = jnp.max(scores, axis=-1, keepdims=True)
            weights = jnp.exp2((scores - top_score) * factor)
            return weights.astype(jnp.bfloat16).reshape(step_rows, scores.shape[2])

        def mix(weights, extended):
            both = jnp.dot(weights, extended, preferred_element_type=jnp.float32)
            return both[:, :value_dim], both[:, value_dim : value_dim + value_dim]

        def some_heads(step, carry):
            here = pl.ds(pl.multiple_of(step * step_rows, step_rows), step_rows)
            query = rows[here, :]
            weights = weigh(contract(query, sel_keys[:, :key_dim]), sel_bias)
            numer, denom = mix(weights, sel_values[...])
            total = gates[1, here, :] * numer / denom
            weights = weigh(contract(query, table[pl.ds(win_start, win_len), :key_dim]), win_bias)
            numer, denom = mix(weights, win_values[...])
            total = total + gates[2, here, :] * numer / denom
            scores = (
                contract(query, comp_parts[0]) + contract(query, comp_parts[1])
            ) + contract(query, comp_parts[2])
            weights = weigh(scores, comp_bias)
            numer, denom = mix(weights, comp_high[...])
            numer = numer + jnp.dot(weights, comp_low[...], preferred_element_type=jnp.float32)
            total = (total + gates[0, here, :] * numer / denom).astype(out.dtype)
            pieces = [total[n * block : (n + 1) * block, :] for n in range(heads_step)]
            columns = pl.ds(pl.multiple_of(step * heads_step * value_dim, LANES), heads_step * value_dim)
            out[top : top + block, columns] = jnp.concatenate(pieces, axis=1)
            return carry

        lax.fori_loop(0, heads // heads_step, some_heads, 0)


def attend(within, stride, key_dim, select, queries, gate_logits, table, comp):
    length = queries.shape[0]
    tiles, picks = select.shape
    block = length // tiles
    heads = gate_logits.shape[1] // 3
    value_dim = table.shape[1] - padded(key_dim)
    comp_count = comp.shape[0]
    win_len = WINDOW + block
    sel_len = picks * block
    vmem = pl.BlockSpec(memory_space=pltpu.VMEM)
    smem = pl.BlockSpec(memory_space=pltpu.SMEM)
    bf16, f32 = jnp.bfloat16, jnp.float32
    return pl.pallas_call(
        functools.partial(attend_kernel, within, stride, key_dim, 4),
        out_shape=jax.ShapeDtypeStruct((length, heads * value_dim), queries.dtype),
        in_specs=[smem, vmem, vmem, vmem, vmem],
        out_specs=vmem,
        scratch_shapes=[
            pltpu.VMEM((heads * block, key_dim), bf16),
            pltpu.VMEM((3, heads * block, LANES), f32),
            pltpu.VMEM((sel_len, padded(key_dim)), bf16),
            pltpu.VMEM((sel_len, value_dim + LANES), bf16),
            pltpu.VMEM((win_len, value_dim + LANES), bf16),
            pltpu.VMEM((3, comp_count, key_dim), bf16),
            pltpu.VMEM((comp_count, value_dim + LANES), bf16),
            pltpu.VMEM((comp_count, value_dim), bf16),
            pltpu.VMEM((block, sel_len), f32),
            pltpu.VMEM((block, win_len), f32),
            pltpu.VMEM((block, comp_count), f32),
        ],
        compiler_params=pltpu.CompilerParams(vmem_limit_bytes=56 * 1024 * 1024),
        name="attend",
    )(select, queries, gate_logits.T, table, comp)


def shards(queries, keys, values, comp_key_weight, comp_value_weight, select, gate_logits):
    groups = lax.axis_size("grp")
    within = lax.axis_size("seq")
    table, comp = exchange(groups, within, keys, values, comp_key_weight, comp_value_weight)
    table = table.reshape(-1, table.shape[2])
    comp = comp.reshape(-1, comp.shape[2])
    return attend(
        within, comp_key_weight.shape[0], keys.shape[1], select, queries, gate_logits, table, comp
    )


def solution(mesh):
    return jax.shard_map(
        shards,
        mesh=mesh,
        in_specs=(
            P(("grp", "seq"), None),
            P(("grp", "seq"), None),
            P(("grp", "seq"), None),
            P(),
            P(),
            P(("grp", "seq"), None),
            P(("grp", "seq"), None),
        ),
        out_specs=P(("grp", "seq"), None),
        check_vma=False,
    )
```

```python
import functools

import jax
import jax.numpy as jnp
from jax import lax
from jax.experimental import pallas as pl
from jax.experimental.pallas import tpu as pltpu
from jax.sharding import PartitionSpec as P

WINDOW = 512
LANES = 128
MESH = pl.DeviceIdType.MESH


def padded(width):
    return -(-width // LANES) * LANES


def fused_kernel(
    groups, within, heads_step, queries, keys_turned, values, key_weight, value_weight, select,
    gate_logits, out, table, comp, recv_rows, recv_comp, along_rows, along_comp,
    pair_rows, pair_comp, next_rows, next_comp,
    rows, gates, total, sel_keys, sel_values, win_values, comp_parts, comp_high, comp_low,
    sel_bias, win_bias, comp_bias,
):
    group = lax.axis_index("grp")
    seq = lax.axis_index("seq")
    half = within // 2
    sibling = seq + 1 - 2 * lax.rem(seq, 2)
    length = values.shape[0]
    key_dim = keys_turned.shape[0]
    key_room = padded(key_dim)
    stride = key_weight.shape[0]
    comp_rows = length // stride
    tiles, picks = select.shape
    block = length // tiles
    heads = gate_logits.shape[0] // 3
    value_dim = values.shape[1]
    comp_count = comp.shape[0]
    win_len = win_bias.shape[2]
    first_block = (group - 1) * within * tiles
    win_blocks = win_len // block
    factor = key_dim ** (-0.5) * 1.4426950408889634
    low = -jnp.inf
    step_rows = heads_step * block
    steps = heads // heads_step

    def table_at(slot):
        return table.at[pl.ds(slot * tiles, tiles)]

    def comp_at(slot):
        return comp.at[pl.ds(pl.multiple_of(slot * comp_rows, comp_rows), comp_rows)]

    def same_parity(distance):
        return lax.rem(seq + 2 * distance + 2 * within, within)

    barrier = pltpu.get_barrier_semaphore()

    def greet(distance, carry):
        pl.semaphore_signal(
            barrier, inc=1, device_id=(group, same_parity(distance)), device_id_type=MESH
        )
        return carry

    lax.fori_loop(1, half, greet, 0)
    pl.semaphore_signal(barrier, inc=1, device_id=(group, sibling), device_id_type=MESH)
    for step in range(1, groups):
        other = lax.rem(group + step, groups)
        pl.semaphore_signal(barrier, inc=1, device_id=(other, seq), device_id_type=MESH)

    own_slot = within + seq
    own_comp = group * within + seq
    own_rows = pl.ds(own_slot * tiles, tiles)
    own_comp_rows = pl.ds(pl.multiple_of(own_comp * comp_rows, comp_rows), comp_rows)
    keys = keys_turned[...].T
    table[own_rows, :, :key_room] = jnp.zeros((tiles, block, key_room), table.dtype)
    table[own_rows, :, :key_dim] = keys.reshape(tiles, block, key_dim)
    table[own_rows, :, key_room:] = values[...].reshape(tiles, block, value_dim)
    comp[own_comp_rows, :] = jnp.zeros((comp_rows, comp.shape[1]), jnp.float32)

    def summed(source, weight):
        wide = source.astype(jnp.float32).reshape(comp_rows, stride, source.shape[1])
        return jnp.sum(wide * weight[...][None], axis=1)

    comp[own_comp_rows, :key_dim] = summed(keys, key_weight)
    comp[own_comp_rows, key_room:] = summed(values[...], value_weight)
    @pl.when(group == 0)
    def _():
        table[: within * tiles] = jnp.zeros((within * tiles, block, table.shape[2]), table.dtype)

    group_comp = within * comp_rows
    for later in range(1, groups):
        @pl.when(group < later)
        def _():
            comp[later * group_comp : (later + 1) * group_comp, :] = jnp.zeros(
                (group_comp, comp.shape[1]), jnp.float32
            )

    pl.semaphore_wait(barrier, half - 1 + 1 + groups - 1)

    def rows_copy(source, slot, send_sem, target):
        return pltpu.make_async_remote_copy(
            src_ref=source, dst_ref=table_at(slot), send_sem=send_sem,
            recv_sem=recv_rows.at[slot], device_id=target, device_id_type=MESH,
        )

    def comp_copy(source, slot, send_sem, target):
        return pltpu.make_async_remote_copy(
            src_ref=source, dst_ref=comp_at(slot), send_sem=send_sem,
            recv_sem=recv_comp.at[slot], device_id=target, device_id_type=MESH,
        )

    def rows_next(source, member):
        @pl.when(group < groups - 1)
        def _():
            rows_copy(source, member, next_rows.at[member], (group + 1, seq)).start()

    def comp_next(source, member):
        for step in range(1, groups):
            @pl.when(group + step < groups)
            def _():
                comp_copy(
                    source, group * within + member,
                    next_comp.at[step * within + member], (group + step, seq),
                ).start()

    packed = table_at(own_slot)
    comp_own = comp_at(own_comp)

    def spread_comp(distance, carry):
        target = (group, same_parity(distance))
        comp_copy(comp_own, own_comp, along_comp.at[distance], target).start()
        return carry

    def spread_rows(distance, carry):
        target = (group, same_parity(distance))
        rows_copy(packed, own_slot, along_rows.at[distance], target).start()
        return carry

    lax.fori_loop(1, half, spread_comp, 0)
    comp_next(comp_own, seq)
    comp_copy(comp_own, own_comp, pair_comp.at[own_comp], (group, sibling)).start()
    lax.fori_loop(1, half, spread_rows, 0)
    rows_next(packed, seq)
    rows_copy(packed, own_slot, pair_rows.at[own_slot], (group, sibling)).start()

    def arrive_rows(slot):
        rows_copy(packed, slot, pair_rows.at[slot], (group, sibling)).wait_recv()

    def arrive_comp(slot):
        comp_copy(comp_own, slot, pair_comp.at[slot], (group, sibling)).wait_recv()

    def stage(tile):
        top = tile * block
        tile_place = (group * within + seq) * length + top
        for head in range(heads):
            rows[tile, head * block : (head + 1) * block, :] = queries[
                top : top + block, head * key_dim : (head + 1) * key_dim
            ]
            for branch in range(3):
                column = branch * heads + head
                gates[tile, branch, head * block : (head + 1) * block, :] = jnp.broadcast_to(
                    gate_all[top : top + block, column : column + 1], (block, LANES)
                )
        lane_all = lax.broadcasted_iota(jnp.int32, (block, picks * block), 1)
        row_place = tile_place + lax.broadcasted_iota(jnp.int32, (block, picks * block), 0)
        shift = jnp.zeros((1, picks * block), jnp.int32)
        lane_one = lax.broadcasted_iota(jnp.int32, (1, picks * block), 1)
        for pick in range(picks):
            inside = (lane_one >= pick * block) & (lane_one < (pick + 1) * block)
            shift = jnp.where(inside, (select[tile, pick] - pick) * block, shift)
        sel_bias[tile] = jnp.where(lane_all + shift <= row_place, 0.0, low)
        win_place = tile_place - (win_len - block) + lax.broadcasted_iota(jnp.int32, (block, win_len), 1)
        win_row = tile_place + lax.broadcasted_iota(jnp.int32, (block, win_len), 0)
        win_bias[tile] = jnp.where(
            (win_place <= win_row) & (win_place > win_row - WINDOW) & (win_place >= 0), 0.0, low
        )
        comp_place = stride * lax.broadcasted_iota(jnp.int32, (block, comp_count), 1)
        comp_row = tile_place + lax.broadcasted_iota(jnp.int32, (block, comp_count), 0)
        comp_bias[tile] = jnp.where(comp_place <= comp_row, 0.0, low)
        sel_values[tile, :, value_dim:] = jnp.ones((picks * block, LANES), jnp.bfloat16)

    def weigh(scores, bias):
        scores = scores.reshape(heads_step, block, scores.shape[1]) + bias[None]
        top_score = jnp.max(scores, axis=-1, keepdims=True)
        weights = jnp.exp2((scores - top_score) * factor)
        return weights.astype(jnp.bfloat16).reshape(step_rows, scores.shape[2])

    def mix(weights, extended):
        both = jnp.dot(weights, extended, preferred_element_type=jnp.float32)
        return both[:, :value_dim], both[:, value_dim : value_dim + value_dim]

    def step_at(step):
        return pl.ds(pl.multiple_of(step * step_rows, step_rows), step_rows)

    def comp_unit(unit, carry):
        tile, here = unit // steps, step_at(unit % steps)
        query = rows[tile, here, :]
        scores = (
            contract(query, comp_parts[0]) + contract(query, comp_parts[1])
        ) + contract(query, comp_parts[2])
        weights = weigh(scores, comp_bias[tile])
        numer, denom = mix(weights, comp_high[...])
        numer = numer + jnp.dot(weights, comp_low[...], preferred_element_type=jnp.float32)
        total[tile, here, :] = gates[tile, 0, here, :] * numer / denom
        return carry

    def relay_comp(distance, carry):
        member = same_parity(-distance)
        slot = group * within + member
        arrive_comp(slot)
        comp_next(comp_at(slot), member)
        comp_copy(comp_at(slot), slot, pair_comp.at[slot], (group, sibling)).start()
        return carry

    def relay_prior_comp(distance, carry):
        member = same_parity(-distance)
        for step in range(1, groups):
            @pl.when(group >= step)
            def _():
                slot = (group - step) * within + member
                arrive_comp(slot)
                comp_copy(comp_at(slot), slot, pair_comp.at[slot], (group, sibling)).start()

        return carry

    def finish_comp(distance, carry):
        other = same_parity(distance) + sibling - seq
        arrive_comp(group * within + other)
        for step in range(1, groups):
            @pl.when(group >= step)
            def _():
                arrive_comp((group - step) * within + other)

        return carry

    def relay_rows(distance):
        member = same_parity(-distance)
        slot = within + member
        arrive_rows(slot)
        rows_next(table_at(slot), member)
        rows_copy(table_at(slot), slot, pair_rows.at[slot], (group, sibling)).start()

    def relay_prior_rows(distance, carry):
        member = same_parity(-distance)

        @pl.when(group > 0)
        def _():
            arrive_rows(member)
            rows_copy(table_at(member), member, pair_rows.at[member], (group, sibling)).start()

        return carry

    def finish_rows(distance, carry):
        other = same_parity(distance) + sibling - seq
        arrive_rows(within + other)

        @pl.when(group > 0)
        def _():
            arrive_rows(other)

        return carry

    gate_all = jax.nn.sigmoid(gate_logits[...]).T
    stage(0)
    lax.fori_loop(1, half, relay_comp, 0)
    for tile in range(1, tiles):
        stage(tile)
    win_values[:, value_dim:] = jnp.ones((win_len, LANES), jnp.bfloat16)
    comp_high[:, value_dim:] = jnp.ones((comp_count, LANES), jnp.bfloat16)
    lax.fori_loop(0, half, relay_prior_comp, 0)
    if half > 1:
        relay_rows(1)
    lax.fori_loop(0, half, finish_comp, 0)
    rest = comp[:, :key_dim]
    for part in range(3):
        piece = rest.astype(jnp.bfloat16)
        comp_parts[part] = piece
        rest = rest - piece.astype(jnp.float32)
    value_part = comp[:, key_room:]
    high = value_part.astype(jnp.bfloat16)
    comp_high[:, :value_dim] = high
    comp_low[...] = (value_part - high.astype(jnp.float32)).astype(jnp.bfloat16)
    units = tiles * steps
    spans = max(half - 1, 1)

    def relay_and_weigh(distance, carry):
        relay_rows(distance)
        lax.fori_loop(units * (distance - 2) // spans, units * (distance - 1) // spans, comp_unit, 0)
        return carry

    lax.fori_loop(2, half, relay_and_weigh, 0)
    lax.fori_loop(units * max(half - 2, 0) // spans, units, comp_unit, 0)
    lax.fori_loop(0, half, relay_prior_rows, 0)
    lax.fori_loop(0, half, finish_rows, 0)

    for tile in range(tiles):
        top = tile * block
        for pick in range(picks):
            got = table[jnp.clip(select[tile, pick] - first_block, 0, 2 * within * tiles - 1)]
            sel_keys[pick * block : (pick + 1) * block, :] = got[:, :key_room]
            sel_values[tile, pick * block : (pick + 1) * block, :value_dim] = got[:, key_room:]
        win_here = pl.ds(within * tiles + seq * tiles + tile - (win_blocks - 1), win_blocks)
        win_values[:, :value_dim] = table[win_here, :, key_room:].reshape(win_len, value_dim)

        def some_heads(step, carry):
            here = step_at(step)
            query = rows[tile, here, :]
            weights = weigh(contract(query, sel_keys[:, :key_dim]), sel_bias[tile])
            numer, denom = mix(weights, sel_values[tile])
            result = total[tile, here, :] + gates[tile, 1, here, :] * numer / denom
            weights = weigh(contract(query, table[win_here, :, :key_dim].reshape(win_len, key_dim)), win_bias[tile])
            numer, denom = mix(weights, win_values[...])
            result = (result + gates[tile, 2, here, :] * numer / denom).astype(out.dtype)
            pieces = [result[n * block : (n + 1) * block, :] for n in range(heads_step)]
            columns = pl.ds(pl.multiple_of(step * heads_step * value_dim, LANES), heads_step * value_dim)
            out[top : top + block, columns] = jnp.concatenate(pieces, axis=1)
            return carry

        lax.fori_loop(0, steps, some_heads, 0)

    def sent_here(distance, carry):
        member = same_parity(distance)
        rows_copy(packed, within + member, pair_rows.at[within + member], (group, sibling)).wait_send()
        comp_copy(
            comp_own, group * within + member, pair_comp.at[group * within + member], (group, sibling)
        ).wait_send()

        @pl.when(group > 0)
        def _():
            rows_copy(packed, member, pair_rows.at[member], (group, sibling)).wait_send()

        @pl.when(group < groups - 1)
        def _():
            rows_copy(packed, member, next_rows.at[member], (group + 1, seq)).wait_send()

        for step in range(1, groups):
            @pl.when(group >= step)
            def _():
                slot = (group - step) * within + member
                comp_copy(comp_own, slot, pair_comp.at[slot], (group, sibling)).wait_send()

            @pl.when(group + step < groups)
            def _():
                comp_copy(
                    comp_own, group * within + member,
                    next_comp.at[step * within + member], (group + step, seq),
                ).wait_send()

        return carry

    lax.fori_loop(0, half, sent_here, 0)

    def sent_along(distance, carry):
        target = (group, same_parity(distance))
        rows_copy(packed, own_slot, along_rows.at[distance], target).wait_send()
        comp_copy(comp_own, own_comp, along_comp.at[distance], target).wait_send()
        return carry

    lax.fori_loop(1, half, sent_along, 0)


def contract(left, right):
    return lax.dot_general(left, right, (((1,), (1,)), ((), ())), preferred_element_type=jnp.float32)


def shards(queries, keys, values, comp_key_weight, comp_value_weight, select, gate_logits):
    groups = lax.axis_size("grp")
    within = lax.axis_size("seq")
    length, key_dim = keys.shape
    value_dim = values.shape[1]
    tiles, picks = select.shape
    block = length // tiles
    heads = gate_logits.shape[1] // 3
    width = padded(key_dim) + padded(value_dim)
    comp_rows = length // comp_key_weight.shape[0]
    comp_count = groups * within * comp_rows
    win_len = WINDOW + block
    sel_len = picks * block
    dma = pltpu.SemaphoreType.DMA
    vmem = pl.BlockSpec(memory_space=pltpu.VMEM)
    smem = pl.BlockSpec(memory_space=pltpu.SMEM)
    bf16, f32 = jnp.bfloat16, jnp.float32
    return pl.pallas_call(
        functools.partial(fused_kernel, groups, within, 4),
        out_shape=jax.ShapeDtypeStruct((length, heads * value_dim), queries.dtype),
        in_specs=[vmem, vmem, vmem, vmem, vmem, smem, vmem],
        out_specs=vmem,
        scratch_shapes=[
            pltpu.VMEM((2 * within * tiles, block, width), bf16),
            pltpu.VMEM((comp_count, width), f32),
            dma((2 * within,)),
            dma((groups * within,)),
            dma((within,)),
            dma((within,)),
            dma((2 * within,)),
            dma((groups * within,)),
            dma((within,)),
            dma((groups * within,)),
            pltpu.VMEM((tiles, heads * block, key_dim), bf16),
            pltpu.VMEM((tiles, 3, heads * block, LANES), f32),
            pltpu.VMEM((tiles, heads * block, value_dim), f32),
            pltpu.VMEM((sel_len, padded(key_dim)), bf16),
            pltpu.VMEM((tiles, sel_len, value_dim + LANES), bf16),
            pltpu.VMEM((win_len, value_dim + LANES), bf16),
            pltpu.VMEM((3, comp_count, key_dim), bf16),
            pltpu.VMEM((comp_count, value_dim + LANES), bf16),
            pltpu.VMEM((comp_count, value_dim), bf16),
            pltpu.VMEM((tiles, block, sel_len), f32),
            pltpu.VMEM((tiles, block, win_len), f32),
            pltpu.VMEM((tiles, block, comp_count), f32),
        ],
        compiler_params=pltpu.CompilerParams(
            collective_id=0, has_side_effects=True, vmem_limit_bytes=56 * 1024 * 1024
        ),
        name="attend",
    )(queries, keys.T, values, comp_key_weight, comp_value_weight, select, gate_logits.T)


def solution(mesh):
    return jax.shard_map(
        shards,
        mesh=mesh,
        in_specs=(
            P(("grp", "seq"), None),
            P(("grp", "seq"), None),
            P(("grp", "seq"), None),
            P(),
            P(),
            P(("grp", "seq"), None),
            P(("grp", "seq"), None),
        ),
        out_specs=P(("grp", "seq"), None),
        check_vma=False,
    )
```

```python
import functools

import jax
import jax.numpy as jnp
from jax import lax
from jax.experimental import pallas as pl
from jax.experimental.pallas import tpu as pltpu
from jax.sharding import PartitionSpec as P

WINDOW = 512
LANES = 128
MESH = pl.DeviceIdType.MESH


def padded(width):
    return -(-width // LANES) * LANES


def fused_kernel(
    groups, within, heads_step, queries, keys_turned, values, key_weight, value_weight, select,
    gate_logits, out, table, comp, recv_rows, recv_comp, along_rows, along_comp,
    pair_rows, pair_comp, next_rows, next_comp,
    rows, gates, total, sel_keys, sel_values, win_values, comp_parts, comp_high, comp_low,
    sel_bias, win_bias, comp_bias,
):
    group = lax.axis_index("grp")
    seq = lax.axis_index("seq")
    half = within // 2
    sibling = seq + 1 - 2 * lax.rem(seq, 2)
    length = values.shape[0]
    key_dim = keys_turned.shape[0]
    key_room = padded(key_dim)
    stride = key_weight.shape[0]
    comp_rows = length // stride
    tiles, picks = select.shape
    block = length // tiles
    heads = gate_logits.shape[0] // 3
    value_dim = values.shape[1]
    comp_count = comp.shape[0]
    win_len = win_bias.shape[2]
    first_block = (group - 1) * within * tiles
    win_blocks = win_len // block
    factor = key_dim ** (-0.5) * 1.4426950408889634
    low = -jnp.inf
    step_rows = heads_step * block
    steps = heads // heads_step

    def table_at(slot):
        return table.at[pl.ds(slot * tiles, tiles)]

    def comp_at(slot):
        return comp.at[pl.ds(pl.multiple_of(slot * comp_rows, comp_rows), comp_rows)]

    def same_parity(distance):
        return lax.rem(seq + 2 * distance + 2 * within, within)

    barrier = pltpu.get_barrier_semaphore()

    def greet(distance, carry):
        pl.semaphore_signal(
            barrier, inc=1, device_id=(group, same_parity(distance)), device_id_type=MESH
        )
        return carry

    lax.fori_loop(1, half, greet, 0)
    pl.semaphore_signal(barrier, inc=1, device_id=(group, sibling), device_id_type=MESH)
    for step in range(1, groups):
        other = lax.rem(group + step, groups)
        pl.semaphore_signal(barrier, inc=1, device_id=(other, seq), device_id_type=MESH)

    own_slot = within + seq
    own_comp = group * within + seq
    own_rows = pl.ds(own_slot * tiles, tiles)
    own_comp_rows = pl.ds(pl.multiple_of(own_comp * comp_rows, comp_rows), comp_rows)
    keys = keys_turned[...].T
    table[own_rows, :, :key_room] = jnp.zeros((tiles, block, key_room), table.dtype)
    table[own_rows, :, :key_dim] = keys.reshape(tiles, block, key_dim)
    table[own_rows, :, key_room:] = values[...].reshape(tiles, block, value_dim)
    comp[own_comp_rows, :] = jnp.zeros((comp_rows, comp.shape[1]), jnp.float32)

    def summed(source, weight):
        wide = source.astype(jnp.float32).reshape(comp_rows, stride, source.shape[1])
        return jnp.sum(wide * weight[...][None], axis=1)

    comp[own_comp_rows, :key_dim] = summed(keys, key_weight)
    comp[own_comp_rows, key_room:] = summed(values[...], value_weight)
    @pl.when(group == 0)
    def _():
        table[: within * tiles] = jnp.zeros((within * tiles, block, table.shape[2]), table.dtype)

    group_comp = within * comp_rows
    for later in range(1, groups):
        @pl.when(group < later)
        def _():
            comp[later * group_comp : (later + 1) * group_comp, :] = jnp.zeros(
                (group_comp, comp.shape[1]), jnp.float32
            )

    pl.semaphore_wait(barrier, half - 1 + 1 + groups - 1)

    def rows_copy(source, slot, send_sem, target):
        return pltpu.make_async_remote_copy(
            src_ref=source, dst_ref=table_at(slot), send_sem=send_sem,
            recv_sem=recv_rows.at[slot], device_id=target, device_id_type=MESH,
        )

    def comp_copy(source, slot, send_sem, target):
        return pltpu.make_async_remote_copy(
            src_ref=source, dst_ref=comp_at(slot), send_sem=send_sem,
            recv_sem=recv_comp.at[slot], device_id=target, device_id_type=MESH,
        )

    def rows_next(source, member):
        @pl.when(group < groups - 1)
        def _():
            rows_copy(source, member, next_rows.at[member], (group + 1, seq)).start()

    def comp_next(source, member):
        for step in range(1, groups):
            @pl.when(group + step < groups)
            def _():
                comp_copy(
                    source, group * within + member,
                    next_comp.at[step * within + member], (group + step, seq),
                ).start()

    packed = table_at(own_slot)
    comp_own = comp_at(own_comp)

    def spread_comp(distance, carry):
        target = (group, same_parity(distance))
        comp_copy(comp_own, own_comp, along_comp.at[distance], target).start()
        return carry

    def spread_rows(distance, carry):
        target = (group, same_parity(distance))
        rows_copy(packed, own_slot, along_rows.at[distance], target).start()
        return carry

    lax.fori_loop(1, half, spread_comp, 0)
    comp_next(comp_own, seq)
    comp_copy(comp_own, own_comp, pair_comp.at[own_comp], (group, sibling)).start()
    lax.fori_loop(1, half, spread_rows, 0)
    rows_next(packed, seq)
    rows_copy(packed, own_slot, pair_rows.at[own_slot], (group, sibling)).start()

    def arrive_rows(slot):
        rows_copy(packed, slot, pair_rows.at[slot], (group, sibling)).wait_recv()

    def arrive_comp(slot):
        comp_copy(comp_own, slot, pair_comp.at[slot], (group, sibling)).wait_recv()

    def stage(tile):
        top = tile * block
        tile_place = (group * within + seq) * length + top
        for head in range(heads):
            rows[tile, head * block : (head + 1) * block, :] = queries[
                top : top + block, head * key_dim : (head + 1) * key_dim
            ]
            for branch in range(3):
                column = branch * heads + head
                gates[tile, branch, head * block : (head + 1) * block, :] = jnp.broadcast_to(
                    gate_all[top : top + block, column : column + 1], (block, LANES)
                )
        lane_all = lax.broadcasted_iota(jnp.int32, (block, picks * block), 1)
        row_place = tile_place + lax.broadcasted_iota(jnp.int32, (block, picks * block), 0)
        shift = jnp.zeros((1, picks * block), jnp.int32)
        lane_one = lax.broadcasted_iota(jnp.int32, (1, picks * block), 1)
        for pick in range(picks):
            inside = (lane_one >= pick * block) & (lane_one < (pick + 1) * block)
            shift = jnp.where(inside, (select[tile, pick] - pick) * block, shift)
        sel_bias[tile] = jnp.where(lane_all + shift <= row_place, 0.0, low)
        win_place = tile_place - (win_len - block) + lax.broadcasted_iota(jnp.int32, (block, win_len), 1)
        win_row = tile_place + lax.broadcasted_iota(jnp.int32, (block, win_len), 0)
        win_bias[tile] = jnp.where(
            (win_place <= win_row) & (win_place > win_row - WINDOW) & (win_place >= 0), 0.0, low
        )
        comp_place = stride * lax.broadcasted_iota(jnp.int32, (block, comp_count), 1)
        comp_row = tile_place + lax.broadcasted_iota(jnp.int32, (block, comp_count), 0)
        comp_bias[tile] = jnp.where(comp_place <= comp_row, 0.0, low)
        sel_values[tile, :, value_dim:] = jnp.ones((picks * block, LANES), jnp.bfloat16)

    def weigh(scores, bias):
        scores = scores.reshape(heads_step, block, scores.shape[1]) + bias[None]
        top_score = jnp.max(scores, axis=-1, keepdims=True)
        weights = jnp.exp2((scores - top_score) * factor)
        return weights.astype(jnp.bfloat16).reshape(step_rows, scores.shape[2])

    def mix(weights, extended):
        both = jnp.dot(weights, extended, preferred_element_type=jnp.float32)
        return both[:, :value_dim], both[:, value_dim : value_dim + value_dim]

    def step_at(step):
        return pl.ds(pl.multiple_of(step * step_rows, step_rows), step_rows)

    def comp_unit(unit, carry):
        tile, here = unit // steps, step_at(unit % steps)
        query = rows[tile, here, :]
        scores = (
            contract(query, comp_parts[0]) + contract(query, comp_parts[1])
        ) + contract(query, comp_parts[2])
        weights = weigh(scores, comp_bias[tile])
        numer, denom = mix(weights, comp_high[...])
        numer = numer + jnp.dot(weights, comp_low[...], preferred_element_type=jnp.float32)
        total[tile, here, :] = gates[tile, 0, here, :] * numer / denom
        return carry

    def relay_comp(distance, carry):
        member = same_parity(-distance)
        slot = group * within + member
        arrive_comp(slot)
        comp_next(comp_at(slot), member)
        comp_copy(comp_at(slot), slot, pair_comp.at[slot], (group, sibling)).start()
        return carry

    def relay_prior_comp(distance, carry):
        member = same_parity(-distance)
        for step in range(1, groups):
            @pl.when(group >= step)
            def _():
                slot = (group - step) * within + member
                arrive_comp(slot)
                comp_copy(comp_at(slot), slot, pair_comp.at[slot], (group, sibling)).start()

        return carry

    def finish_comp(distance, carry):
        other = same_parity(distance) + sibling - seq
        arrive_comp(group * within + other)
        for step in range(1, groups):
            @pl.when(group >= step)
            def _():
                arrive_comp((group - step) * within + other)

        return carry

    def relay_rows(distance):
        member = same_parity(-distance)
        slot = within + member
        arrive_rows(slot)
        rows_next(table_at(slot), member)
        rows_copy(table_at(slot), slot, pair_rows.at[slot], (group, sibling)).start()

    def relay_prior_rows(distance, carry):
        member = same_parity(-distance)

        @pl.when(group > 0)
        def _():
            arrive_rows(member)
            rows_copy(table_at(member), member, pair_rows.at[member], (group, sibling)).start()

        return carry

    def finish_rows(distance, carry):
        other = same_parity(distance) + sibling - seq
        arrive_rows(within + other)

        @pl.when(group > 0)
        def _():
            arrive_rows(other)

        return carry

    gate_all = jax.nn.sigmoid(gate_logits[...]).T
    stage(0)
    lax.fori_loop(1, half, relay_comp, 0)
    for tile in range(1, tiles):
        stage(tile)
    win_values[:, value_dim:] = jnp.ones((win_len, LANES), jnp.bfloat16)
    comp_high[:, value_dim:] = jnp.ones((comp_count, LANES), jnp.bfloat16)

    def relay_near(distance, carry):
        relay_rows(distance)
        return carry

    lax.fori_loop(1, half, relay_near, 0)
    lax.fori_loop(0, half, relay_prior_comp, 0)
    lax.fori_loop(0, half, finish_comp, 0)
    rest = comp[:, :key_dim]
    for part in range(3):
        piece = rest.astype(jnp.bfloat16)
        comp_parts[part] = piece
        rest = rest - piece.astype(jnp.float32)
    value_part = comp[:, key_room:]
    high = value_part.astype(jnp.bfloat16)
    comp_high[:, :value_dim] = high
    comp_low[...] = (value_part - high.astype(jnp.float32)).astype(jnp.bfloat16)
    units = tiles * steps

    def relay_and_weigh(distance, carry):
        lax.fori_loop(units * distance // half, units * (distance + 1) // half, comp_unit, 0)
        return relay_prior_rows(distance, carry)

    lax.fori_loop(0, half, relay_and_weigh, 0)
    lax.fori_loop(0, half, finish_rows, 0)

    for tile in range(tiles):
        top = tile * block
        for pick in range(picks):
            got = table[jnp.clip(select[tile, pick] - first_block, 0, 2 * within * tiles - 1)]
            sel_keys[pick * block : (pick + 1) * block, :] = got[:, :key_room]
            sel_values[tile, pick * block : (pick + 1) * block, :value_dim] = got[:, key_room:]
        win_here = pl.ds(within * tiles + seq * tiles + tile - (win_blocks - 1), win_blocks)
        win_values[:, :value_dim] = table[win_here, :, key_room:].reshape(win_len, value_dim)

        def some_heads(step, carry):
            here = step_at(step)
            query = rows[tile, here, :]
            weights = weigh(contract(query, sel_keys[:, :key_dim]), sel_bias[tile])
            numer, denom = mix(weights, sel_values[tile])
            result = total[tile, here, :] + gates[tile, 1, here, :] * numer / denom
            weights = weigh(contract(query, table[win_here, :, :key_dim].reshape(win_len, key_dim)), win_bias[tile])
            numer, denom = mix(weights, win_values[...])
            result = (result + gates[tile, 2, here, :] * numer / denom).astype(out.dtype)
            pieces = [result[n * block : (n + 1) * block, :] for n in range(heads_step)]
            columns = pl.ds(pl.multiple_of(step * heads_step * value_dim, LANES), heads_step * value_dim)
            out[top : top + block, columns] = jnp.concatenate(pieces, axis=1)
            return carry

        lax.fori_loop(0, steps, some_heads, 0)

    def sent_here(distance, carry):
        member = same_parity(distance)
        rows_copy(packed, within + member, pair_rows.at[within + member], (group, sibling)).wait_send()
        comp_copy(
            comp_own, group * within + member, pair_comp.at[group * within + member], (group, sibling)
        ).wait_send()

        @pl.when(group > 0)
        def _():
            rows_copy(packed, member, pair_rows.at[member], (group, sibling)).wait_send()

        @pl.when(group < groups - 1)
        def _():
            rows_copy(packed, member, next_rows.at[member], (group + 1, seq)).wait_send()

        for step in range(1, groups):
            @pl.when(group >= step)
            def _():
                slot = (group - step) * within + member
                comp_copy(comp_own, slot, pair_comp.at[slot], (group, sibling)).wait_send()

            @pl.when(group + step < groups)
            def _():
                comp_copy(
                    comp_own, group * within + member,
                    next_comp.at[step * within + member], (group + step, seq),
                ).wait_send()

        return carry

    lax.fori_loop(0, half, sent_here, 0)

    def sent_along(distance, carry):
        target = (group, same_parity(distance))
        rows_copy(packed, own_slot, along_rows.at[distance], target).wait_send()
        comp_copy(comp_own, own_comp, along_comp.at[distance], target).wait_send()
        return carry

    lax.fori_loop(1, half, sent_along, 0)


def contract(left, right):
    return lax.dot_general(left, right, (((1,), (1,)), ((), ())), preferred_element_type=jnp.float32)


def shards(queries, keys, values, comp_key_weight, comp_value_weight, select, gate_logits):
    groups = lax.axis_size("grp")
    within = lax.axis_size("seq")
    length, key_dim = keys.shape
    value_dim = values.shape[1]
    tiles, picks = select.shape
    block = length // tiles
    heads = gate_logits.shape[1] // 3
    width = padded(key_dim) + padded(value_dim)
    comp_rows = length // comp_key_weight.shape[0]
    comp_count = groups * within * comp_rows
    win_len = WINDOW + block
    sel_len = picks * block
    dma = pltpu.SemaphoreType.DMA
    vmem = pl.BlockSpec(memory_space=pltpu.VMEM)
    smem = pl.BlockSpec(memory_space=pltpu.SMEM)
    bf16, f32 = jnp.bfloat16, jnp.float32
    return pl.pallas_call(
        functools.partial(fused_kernel, groups, within, 8),
        out_shape=jax.ShapeDtypeStruct((length, heads * value_dim), queries.dtype),
        in_specs=[vmem, vmem, vmem, vmem, vmem, smem, vmem],
        out_specs=vmem,
        scratch_shapes=[
            pltpu.VMEM((2 * within * tiles, block, width), bf16),
            pltpu.VMEM((comp_count, width), f32),
            dma((2 * within,)),
            dma((groups * within,)),
            dma((within,)),
            dma((within,)),
            dma((2 * within,)),
            dma((groups * within,)),
            dma((within,)),
            dma((groups * within,)),
            pltpu.VMEM((tiles, heads * block, key_dim), bf16),
            pltpu.VMEM((tiles, 3, heads * block, LANES), f32),
            pltpu.VMEM((tiles, heads * block, value_dim), f32),
            pltpu.VMEM((sel_len, padded(key_dim)), bf16),
            pltpu.VMEM((tiles, sel_len, value_dim + LANES), bf16),
            pltpu.VMEM((win_len, value_dim + LANES), bf16),
            pltpu.VMEM((3, comp_count, key_dim), bf16),
            pltpu.VMEM((comp_count, value_dim + LANES), bf16),
            pltpu.VMEM((comp_count, value_dim), bf16),
            pltpu.VMEM((tiles, block, sel_len), f32),
            pltpu.VMEM((tiles, block, win_len), f32),
            pltpu.VMEM((tiles, block, comp_count), f32),
        ],
        compiler_params=pltpu.CompilerParams(
            collective_id=0, has_side_effects=True, vmem_limit_bytes=56 * 1024 * 1024
        ),
        name="attend",
    )(queries, keys.T, values, comp_key_weight, comp_value_weight, select, gate_logits.T)


def solution(mesh):
    return jax.shard_map(
        shards,
        mesh=mesh,
        in_specs=(
            P(("grp", "seq"), None),
            P(("grp", "seq"), None),
            P(("grp", "seq"), None),
            P(),
            P(),
            P(("grp", "seq"), None),
            P(("grp", "seq"), None),
        ),
        out_specs=P(("grp", "seq"), None),
        check_vma=False,
    )
```

```python
import functools

import jax
import jax.numpy as jnp
from jax import lax
from jax.experimental import pallas as pl
from jax.experimental.pallas import tpu as pltpu
from jax.sharding import PartitionSpec as P

WINDOW = 512
LANES = 128
MESH = pl.DeviceIdType.MESH


def padded(width):
    return -(-width // LANES) * LANES


def fused_kernel(
    groups, within, heads_step, queries, keys_turned, values, key_weight, value_weight, select,
    gate_logits, out, table, comp, recv_rows, recv_comp, along_rows, along_comp,
    pair_rows, pair_comp, next_rows, next_comp,
    rows, gates, total, sel_keys, sel_values, win_values, comp_parts, comp_high, comp_low,
    sel_bias, win_bias, comp_bias,
):
    group = lax.axis_index("grp")
    seq = lax.axis_index("seq")
    half = within // 2
    sibling = seq + 1 - 2 * lax.rem(seq, 2)
    length = values.shape[0]
    key_dim = keys_turned.shape[0]
    key_room = padded(key_dim)
    stride = key_weight.shape[0]
    comp_rows = length // stride
    tiles, picks = select.shape
    block = length // tiles
    heads = gate_logits.shape[0] // 3
    value_dim = values.shape[1]
    comp_count = comp.shape[0]
    win_len = win_bias.shape[2]
    first_block = (group - 1) * within * tiles
    win_blocks = win_len // block
    factor = key_dim ** (-0.5) * 1.4426950408889634
    low = -jnp.inf
    step_rows = heads_step * block
    steps = heads // heads_step

    def table_at(slot):
        return table.at[pl.ds(slot * tiles, tiles)]

    def comp_at(slot):
        return comp.at[pl.ds(pl.multiple_of(slot * comp_rows, comp_rows), comp_rows)]

    def same_parity(distance):
        return lax.rem(seq + 2 * distance + 2 * within, within)

    barrier = pltpu.get_barrier_semaphore()

    def greet(distance, carry):
        pl.semaphore_signal(
            barrier, inc=1, device_id=(group, same_parity(distance)), device_id_type=MESH
        )
        return carry

    lax.fori_loop(1, half, greet, 0)
    pl.semaphore_signal(barrier, inc=1, device_id=(group, sibling), device_id_type=MESH)
    for step in range(1, groups):
        other = lax.rem(group + step, groups)
        pl.semaphore_signal(barrier, inc=1, device_id=(other, seq), device_id_type=MESH)

    own_slot = within + seq
    own_comp = group * within + seq
    own_rows = pl.ds(own_slot * tiles, tiles)
    own_comp_rows = pl.ds(pl.multiple_of(own_comp * comp_rows, comp_rows), comp_rows)
    keys = keys_turned[...].T
    table[own_rows, :, :key_room] = jnp.zeros((tiles, block, key_room), table.dtype)
    table[own_rows, :, :key_dim] = keys.reshape(tiles, block, key_dim)
    table[own_rows, :, key_room:] = values[...].reshape(tiles, block, value_dim)
    comp[own_comp_rows, :] = jnp.zeros((comp_rows, comp.shape[1]), jnp.float32)

    def summed(source, weight):
        wide = source.astype(jnp.float32).reshape(comp_rows, stride, source.shape[1])
        return jnp.sum(wide * weight[...][None], axis=1)

    comp[own_comp_rows, :key_dim] = summed(keys, key_weight)
    comp[own_comp_rows, key_room:] = summed(values[...], value_weight)
    @pl.when(group == 0)
    def _():
        table[: within * tiles] = jnp.zeros((within * tiles, block, table.shape[2]), table.dtype)

    group_comp = within * comp_rows
    for later in range(1, groups):
        @pl.when(group < later)
        def _():
            comp[later * group_comp : (later + 1) * group_comp, :] = jnp.zeros(
                (group_comp, comp.shape[1]), jnp.float32
            )

    pl.semaphore_wait(barrier, half - 1 + 1 + groups - 1)

    def rows_copy(source, slot, send_sem, target):
        return pltpu.make_async_remote_copy(
            src_ref=source, dst_ref=table_at(slot), send_sem=send_sem,
            recv_sem=recv_rows.at[slot], device_id=target, device_id_type=MESH,
        )

    def comp_copy(source, slot, send_sem, target):
        return pltpu.make_async_remote_copy(
            src_ref=source, dst_ref=comp_at(slot), send_sem=send_sem,
            recv_sem=recv_comp.at[slot], device_id=target, device_id_type=MESH,
        )

    def rows_next(source, member):
        @pl.when(group < groups - 1)
        def _():
            rows_copy(source, member, next_rows.at[member], (group + 1, seq)).start()

    def comp_next(source, member):
        for step in range(1, groups):
            @pl.when(group + step < groups)
            def _():
                comp_copy(
                    source, group * within + member,
                    next_comp.at[step * within + member], (group + step, seq),
                ).start()

    packed = table_at(own_slot)
    comp_own = comp_at(own_comp)

    def spread_comp(distance, carry):
        target = (group, same_parity(distance))
        comp_copy(comp_own, own_comp, along_comp.at[distance], target).start()
        return carry

    def spread_rows(distance, carry):
        target = (group, same_parity(distance))
        rows_copy(packed, own_slot, along_rows.at[distance], target).start()
        return carry

    lax.fori_loop(1, half, spread_comp, 0)
    comp_next(comp_own, seq)
    comp_copy(comp_own, own_comp, pair_comp.at[own_comp], (group, sibling)).start()
    lax.fori_loop(1, half, spread_rows, 0)
    rows_next(packed, seq)
    rows_copy(packed, own_slot, pair_rows.at[own_slot], (group, sibling)).start()

    def arrive_rows(slot):
        rows_copy(packed, slot, pair_rows.at[slot], (group, sibling)).wait_recv()

    def arrive_comp(slot):
        comp_copy(comp_own, slot, pair_comp.at[slot], (group, sibling)).wait_recv()

    def stage(tile):
        top = tile * block
        tile_place = (group * within + seq) * length + top
        for head in range(heads):
            rows[tile, head * block : (head + 1) * block, :] = queries[
                top : top + block, head * key_dim : (head + 1) * key_dim
            ]
            for branch in range(3):
                column = branch * heads + head
                gates[tile, branch, head * block : (head + 1) * block, :] = jnp.broadcast_to(
                    gate_all[top : top + block, column : column + 1], (block, LANES)
                )
        lane_all = lax.broadcasted_iota(jnp.int32, (block, picks * block), 1)
        row_place = tile_place + lax.broadcasted_iota(jnp.int32, (block, picks * block), 0)
        shift = jnp.zeros((1, picks * block), jnp.int32)
        lane_one = lax.broadcasted_iota(jnp.int32, (1, picks * block), 1)
        for pick in range(picks):
            inside = (lane_one >= pick * block) & (lane_one < (pick + 1) * block)
            shift = jnp.where(inside, (select[tile, pick] - pick) * block, shift)
        sel_bias[tile] = jnp.where(lane_all + shift <= row_place, 0.0, low)
        win_place = tile_place - (win_len - block) + lax.broadcasted_iota(jnp.int32, (block, win_len), 1)
        win_row = tile_place + lax.broadcasted_iota(jnp.int32, (block, win_len), 0)
        win_bias[tile] = jnp.where(
            (win_place <= win_row) & (win_place > win_row - WINDOW) & (win_place >= 0), 0.0, low
        )
        comp_place = stride * lax.broadcasted_iota(jnp.int32, (block, comp_count), 1)
        comp_row = tile_place + lax.broadcasted_iota(jnp.int32, (block, comp_count), 0)
        comp_bias[tile] = jnp.where(comp_place <= comp_row, 0.0, low)
        sel_values[tile, :, value_dim:] = jnp.ones((picks * block, LANES), jnp.bfloat16)

    def weigh(scores, bias):
        scores = scores.reshape(heads_step, block, scores.shape[1]) + bias[None]
        top_score = jnp.max(scores, axis=-1, keepdims=True)
        weights = jnp.exp2((scores - top_score) * factor)
        return weights.astype(jnp.bfloat16).reshape(step_rows, scores.shape[2])

    def mix(weights, extended):
        both = jnp.dot(weights, extended, preferred_element_type=jnp.float32)
        return both[:, :value_dim], both[:, value_dim : value_dim + value_dim]

    def step_at(step):
        return pl.ds(pl.multiple_of(step * step_rows, step_rows), step_rows)

    def comp_unit(unit, carry):
        tile, here = unit // steps, step_at(unit % steps)
        query = rows[tile, here, :]
        scores = (
            contract(query, comp_parts[0]) + contract(query, comp_parts[1])
        ) + contract(query, comp_parts[2])
        weights = weigh(scores, comp_bias[tile])
        numer, denom = mix(weights, comp_high[...])
        numer = numer + jnp.dot(weights, comp_low[...], preferred_element_type=jnp.float32)
        total[tile, here, :] = gates[tile, 0, here, :] * numer / denom
        return carry

    def relay_comp(distance, carry):
        member = same_parity(-distance)
        slot = group * within + member
        arrive_comp(slot)
        comp_next(comp_at(slot), member)
        comp_copy(comp_at(slot), slot, pair_comp.at[slot], (group, sibling)).start()
        return carry

    def relay_prior_comp(distance, carry):
        member = same_parity(-distance)
        for step in range(1, groups):
            @pl.when(group >= step)
            def _():
                slot = (group - step) * within + member
                arrive_comp(slot)
                comp_copy(comp_at(slot), slot, pair_comp.at[slot], (group, sibling)).start()

        return carry

    def finish_comp(distance, carry):
        other = same_parity(distance) + sibling - seq
        arrive_comp(group * within + other)
        for step in range(1, groups):
            @pl.when(group >= step)
            def _():
                arrive_comp((group - step) * within + other)

        return carry

    def relay_rows(distance):
        member = same_parity(-distance)
        slot = within + member
        arrive_rows(slot)
        rows_next(table_at(slot), member)
        rows_copy(table_at(slot), slot, pair_rows.at[slot], (group, sibling)).start()

    def relay_prior_rows(distance, carry):
        member = same_parity(-distance)

        @pl.when(group > 0)
        def _():
            arrive_rows(member)
            rows_copy(table_at(member), member, pair_rows.at[member], (group, sibling)).start()

        return carry

    def finish_rows(distance, carry):
        other = same_parity(distance) + sibling - seq
        arrive_rows(within + other)

        @pl.when(group > 0)
        def _():
            arrive_rows(other)

        return carry

    gate_all = jax.nn.sigmoid(gate_logits[...]).T
    stage(0)
    lax.fori_loop(1, half, relay_comp, 0)
    for tile in range(1, tiles):
        stage(tile)
    win_values[:, value_dim:] = jnp.ones((win_len, LANES), jnp.bfloat16)
    comp_high[:, value_dim:] = jnp.ones((comp_count, LANES), jnp.bfloat16)

    def relay_near(distance, carry):
        relay_rows(distance)
        return carry

    lax.fori_loop(1, half, relay_near, 0)
    lax.fori_loop(0, half, relay_prior_comp, 0)
    lax.fori_loop(0, half, finish_comp, 0)
    rest = comp[:, :key_dim]
    for part in range(3):
        piece = rest.astype(jnp.bfloat16)
        comp_parts[part] = piece
        rest = rest - piece.astype(jnp.float32)
    value_part = comp[:, key_room:]
    high = value_part.astype(jnp.bfloat16)
    comp_high[:, :value_dim] = high
    comp_low[...] = (value_part - high.astype(jnp.float32)).astype(jnp.bfloat16)
    units = tiles * steps

    def relay_and_weigh(distance, carry):
        relay_prior_rows(distance, carry)
        return lax.fori_loop(units * distance // half, units * (distance + 1) // half, comp_unit, carry)

    lax.fori_loop(0, half, relay_and_weigh, 0)
    lax.fori_loop(0, half, finish_rows, 0)

    for tile in range(tiles):
        top = tile * block
        for pick in range(picks):
            got = table[jnp.clip(select[tile, pick] - first_block, 0, 2 * within * tiles - 1)]
            sel_keys[pick * block : (pick + 1) * block, :] = got[:, :key_room]
            sel_values[tile, pick * block : (pick + 1) * block, :value_dim] = got[:, key_room:]
        win_here = pl.ds(within * tiles + seq * tiles + tile - (win_blocks - 1), win_blocks)
        win_values[:, :value_dim] = table[win_here, :, key_room:].reshape(win_len, value_dim)

        def some_heads(step, carry):
            here = step_at(step)
            query = rows[tile, here, :]
            weights = weigh(contract(query, sel_keys[:, :key_dim]), sel_bias[tile])
            numer, denom = mix(weights, sel_values[tile])
            result = total[tile, here, :] + gates[tile, 1, here, :] * numer / denom
            weights = weigh(contract(query, table[win_here, :, :key_dim].reshape(win_len, key_dim)), win_bias[tile])
            numer, denom = mix(weights, win_values[...])
            result = (result + gates[tile, 2, here, :] * numer / denom).astype(out.dtype)
            pieces = [result[n * block : (n + 1) * block, :] for n in range(heads_step)]
            columns = pl.ds(pl.multiple_of(step * heads_step * value_dim, LANES), heads_step * value_dim)
            out[top : top + block, columns] = jnp.concatenate(pieces, axis=1)
            return carry

        lax.fori_loop(0, steps, some_heads, 0)

    def sent_here(distance, carry):
        member = same_parity(distance)
        rows_copy(packed, within + member, pair_rows.at[within + member], (group, sibling)).wait_send()
        comp_copy(
            comp_own, group * within + member, pair_comp.at[group * within + member], (group, sibling)
        ).wait_send()

        @pl.when(group > 0)
        def _():
            rows_copy(packed, member, pair_rows.at[member], (group, sibling)).wait_send()

        @pl.when(group < groups - 1)
        def _():
            rows_copy(packed, member, next_rows.at[member], (group + 1, seq)).wait_send()

        for step in range(1, groups):
            @pl.when(group >= step)
            def _():
                slot = (group - step) * within + member
                comp_copy(comp_own, slot, pair_comp.at[slot], (group, sibling)).wait_send()

            @pl.when(group + step < groups)
            def _():
                comp_copy(
                    comp_own, group * within + member,
                    next_comp.at[step * within + member], (group + step, seq),
                ).wait_send()

        return carry

    lax.fori_loop(0, half, sent_here, 0)

    def sent_along(distance, carry):
        target = (group, same_parity(distance))
        rows_copy(packed, own_slot, along_rows.at[distance], target).wait_send()
        comp_copy(comp_own, own_comp, along_comp.at[distance], target).wait_send()
        return carry

    lax.fori_loop(1, half, sent_along, 0)


def contract(left, right):
    return lax.dot_general(left, right, (((1,), (1,)), ((), ())), preferred_element_type=jnp.float32)


def shards(queries, keys, values, comp_key_weight, comp_value_weight, select, gate_logits):
    groups = lax.axis_size("grp")
    within = lax.axis_size("seq")
    length, key_dim = keys.shape
    value_dim = values.shape[1]
    tiles, picks = select.shape
    block = length // tiles
    heads = gate_logits.shape[1] // 3
    width = padded(key_dim) + padded(value_dim)
    comp_rows = length // comp_key_weight.shape[0]
    comp_count = groups * within * comp_rows
    win_len = WINDOW + block
    sel_len = picks * block
    dma = pltpu.SemaphoreType.DMA
    vmem = pl.BlockSpec(memory_space=pltpu.VMEM)
    smem = pl.BlockSpec(memory_space=pltpu.SMEM)
    bf16, f32 = jnp.bfloat16, jnp.float32
    return pl.pallas_call(
        functools.partial(fused_kernel, groups, within, 16),
        out_shape=jax.ShapeDtypeStruct((length, heads * value_dim), queries.dtype),
        in_specs=[vmem, vmem, vmem, vmem, vmem, smem, vmem],
        out_specs=vmem,
        scratch_shapes=[
            pltpu.VMEM((2 * within * tiles, block, width), bf16),
            pltpu.VMEM((comp_count, width), f32),
            dma((2 * within,)),
            dma((groups * within,)),
            dma((within,)),
            dma((within,)),
            dma((2 * within,)),
            dma((groups * within,)),
            dma((within,)),
            dma((groups * within,)),
            pltpu.VMEM((tiles, heads * block, key_dim), bf16),
            pltpu.VMEM((tiles, 3, heads * block, LANES), f32),
            pltpu.VMEM((tiles, heads * block, value_dim), f32),
            pltpu.VMEM((sel_len, padded(key_dim)), bf16),
            pltpu.VMEM((tiles, sel_len, value_dim + LANES), bf16),
            pltpu.VMEM((win_len, value_dim + LANES), bf16),
            pltpu.VMEM((3, comp_count, key_dim), bf16),
            pltpu.VMEM((comp_count, value_dim + LANES), bf16),
            pltpu.VMEM((comp_count, value_dim), bf16),
            pltpu.VMEM((tiles, block, sel_len), f32),
            pltpu.VMEM((tiles, block, win_len), f32),
            pltpu.VMEM((tiles, block, comp_count), f32),
        ],
        compiler_params=pltpu.CompilerParams(
            collective_id=0, has_side_effects=True, vmem_limit_bytes=56 * 1024 * 1024
        ),
        name="attend",
    )(queries, keys.T, values, comp_key_weight, comp_value_weight, select, gate_logits.T)


def solution(mesh):
    return jax.shard_map(
        shards,
        mesh=mesh,
        in_specs=(
            P(("grp", "seq"), None),
            P(("grp", "seq"), None),
            P(("grp", "seq"), None),
            P(),
            P(),
            P(("grp", "seq"), None),
            P(("grp", "seq"), None),
        ),
        out_specs=P(("grp", "seq"), None),
        check_vma=False,
    )
```
